768 devices in a mesh: group: 96 (over z, y), member: 8 (over x, core).
Axes of the slice: x: 4, y: 8, z: 12, core: 2. Of those that a mesh axis runs over, the one named last changes fastest.
Arguments:
- hot_table: bfloat16 [1024, 128], replicated, may hold values from -6 to 6
- warm_table: bfloat16 [8192, 128], P('member'), may hold values from -6 to 6
- cold_table: bfloat16 [98304, 128], P('group'), may hold values from -6 to 6
- warm_serve: int32 [96, 8, 8, 64], P('group', 'member'), may hold values from 0 to 1023
- cold_serve: int32 [96, 8, 96, 2], P('group', 'member'), may hold values from 0 to 1023
- feature_ids: int32 [196608, 20], P(('group', 'member')), may hold values from 0 to 1727, as said below
- labels: int32 [196608], P(('group', 'member')), may hold values 0 or 1
- cross_v: bfloat16 [2560, 256], replicated, may hold values from -0.125 to 0.125
- cross_u: bfloat16 [256, 2560], replicated, may hold values from -0.375 to 0.375
- cross_bias: float32 [2560], replicated, may hold values from -3 to 3
- w_in: bfloat16 [2560, 1024], replicated, may hold values from -0.125 to 0.125
- b_in: float32 [1024], replicated, may hold values from -3 to 3
- w_out: bfloat16 [1024], replicated, may hold values from -0.1875 to 0.1875
Outputs:
- hot_grad: float32 [1024, 128], replicated
- warm_grad: float32 [8192, 128], P('member')
- cold_grad: float32 [98304, 128], P('group')
The draws below stay inside these ranges and needn't reach their ends.
Inputs may be any that keep to these rules, and one draw needn't show every extreme that they name: `feature_ids`: every row of each device's buffer past the hot rows is named by some lookup of that device.
All inputs are finite; a program needn't handle non-finite values. No bound on the sum of `labels` on one device may be relied on, other than what follows from the above.
Results may differ from the reference program's by a relative error of at most 0.006.
Values may be sent and summed in bfloat16 or wider, within the bound.
No kernel may reach another device: no remote copies, remote signals or barrier semaphores. Data moves between devices by JAX's collectives and lax.ppermute only.
A program may use at most 64 MiB of HBM per device.

```python
import jax
import jax.numpy as jnp
from jax import lax

E = 128
F = 20
RANK = 256
HID = 1024
B_DEV = 256
H = 1024
WDEV = 1024
CDEV = 1024
WCAP = 64
CCAP = 2
SAMPLES = 196608
WARM = 8192
COLD = 98304
N_GROUP = 96
N_MEMBER = 8


def draw_feature_ids(key, part):
    key = jax.random.fold_in(key, 11)
    slot_count = N_MEMBER * WCAP + N_GROUP * CCAP
    lookups = B_DEV * F
    device_keys = jax.random.split(key, N_GROUP * N_MEMBER)

    def draw_device(dev_key):
        first_key, second_key = jax.random.split(dev_key)
        filler = jax.random.randint(first_key, (lookups - slot_count,), 0, H)
        needed = H + jnp.arange(slot_count, dtype=jnp.int32)
        combined = jnp.concatenate([needed, filler.astype(jnp.int32)])
        return jax.random.permutation(second_key, combined)
    shuffled = jax.vmap(draw_device)(device_keys)
    return shuffled.reshape(N_GROUP * N_MEMBER * B_DEV, F).astype(jnp.int32)


def place_ends(values, stream_key, least, top_value):
    longest = values.shape.index(max(values.shape))
    spots = []
    for shift in (0, 1):
        where = [jax.random.randint(jax.random.fold_in(stream_key, axis), (), 0, length) for axis, length in enumerate(values.shape)]
        where[longest] = (where[longest] + shift) % values.shape[longest]
        spots.append(tuple(where))
    return values.at[spots[0]].set(least).at[spots[1]].set(top_value)


def levels(own_key, dims, cuts, low, largest):
    loudness, own = 1.0, jax.random.fold_in(own_key, 6)
    for axis_at, shards_of in cuts:
        draws = jnp.exp(jax.random.uniform(jax.random.fold_in(own, axis_at), (shards_of,), jnp.float32, low / len(cuts), largest / len(cuts)))
        loudness = loudness * jnp.repeat(draws, dims[axis_at] // shards_of).reshape([-1 if axis == axis_at else 1 for axis in range(len(dims))])
    return loudness


def normal_values(rng, shape, deviation, most, cuts=(), kind=jnp.bfloat16):
    entries = jax.random.normal(rng, shape, jnp.float32) * deviation
    if len(cuts) > 0:
        entries = levels(rng, shape, cuts, -0.22, 0.18) * entries
    return jnp.clip(entries, min=-most, max=most).astype(kind)


def setup_inputs(seed: int = 0) -> dict:
    arg_keys = jax.random.split(jax.random.key(seed), 14)
    hot_table = normal_values(arg_keys[0], (H, E), 1.0, 6.0)
    warm_table = normal_values(arg_keys[1], (WARM, E), 1.0, 6.0, ((0, 8),))
    cold_table = normal_values(arg_keys[2], (COLD, E), 1.0, 6.0, ((0, 96),))
    warm_serve = place_ends(jax.random.randint(arg_keys[3], (N_GROUP, N_MEMBER, N_MEMBER, WCAP), 0, WDEV), jax.random.fold_in(arg_keys[3], 1), 0, WDEV - 1).astype(jnp.int32)
    cold_serve = place_ends(jax.random.randint(arg_keys[4], (N_GROUP, N_MEMBER, N_GROUP, CCAP), 0, CDEV), jax.random.fold_in(arg_keys[4], 1), 0, CDEV - 1).astype(jnp.int32)
    feature_ids = draw_feature_ids(jax.random.fold_in(arg_keys[13], 71), 0)
    labels = place_ends((jax.random.randint(arg_keys[6], (SAMPLES,), 0, 2) < 1).astype(jnp.int32), jax.random.fold_in(arg_keys[6], 1), 0, 1)
    cross_v = normal_values(arg_keys[7], (F * E, RANK), (F * E) ** -0.5, 0.125)
    cross_u = normal_values(arg_keys[8], (RANK, F * E), RANK ** -0.5, 0.375)
    cross_bias = normal_values(arg_keys[9], (F * E,), 0.5, 3.0, (), jnp.float32)
    w_in = normal_values(arg_keys[10], (F * E, HID), (F * E) ** -0.5, 0.125)
    b_in = normal_values(arg_keys[11], (HID,), 0.5, 3.0, (), jnp.float32)
    w_out = normal_values(arg_keys[12], (HID,), HID ** -0.5, 0.1875)
    return dict(hot_table=hot_table, warm_table=warm_table, cold_table=cold_table, warm_serve=warm_serve, cold_serve=cold_serve, feature_ids=feature_ids, labels=labels, cross_v=cross_v, cross_u=cross_u, cross_bias=cross_bias, w_in=w_in, b_in=b_in, w_out=w_out)


def sample_grads(buffer, row_ids, target, cross_v, cross_u, cross_bias, w_in, b_in, w_out):
    batch_size = row_ids.shape[0]
    inputs = buffer[row_ids.reshape(-1)].reshape(batch_size, -1)
    inputs_f = inputs.astype(jnp.float32)
    narrow = jnp.dot(inputs, cross_v, preferred_element_type=jnp.float32).astype(jnp.bfloat16)
    crossed = jnp.dot(narrow, cross_u, preferred_element_type=jnp.float32) + cross_bias
    layer_one = (inputs_f * crossed + inputs_f).astype(jnp.bfloat16)
    preact = jnp.dot(layer_one, w_in, preferred_element_type=jnp.float32) + b_in
    hidden = jax.nn.silu(preact).astype(jnp.bfloat16)
    logits = jnp.dot(hidden, w_out, preferred_element_type=jnp.float32)
    d_logit = jax.nn.sigmoid(logits) - target
    gate_s = jax.nn.sigmoid(preact)
    d_hidden = (d_logit[:, None] * w_out.astype(jnp.float32)[None, :] * gate_s * (1.0 + preact * (1.0 - gate_s))).astype(jnp.bfloat16)
    d_layer = jnp.dot(d_hidden, w_in.T, preferred_element_type=jnp.float32)
    d_crossed = (d_layer * inputs_f).astype(jnp.bfloat16)
    d_narrow = jnp.dot(d_crossed, cross_u.T, preferred_element_type=jnp.float32).astype(jnp.bfloat16)
    d_inputs = d_layer * (crossed + 1.0) + jnp.dot(d_narrow, cross_v.T, preferred_element_type=jnp.float32)
    return d_inputs.reshape(-1, buffer.shape[1])


def reference(hot_table, warm_table, cold_table, warm_serve, cold_serve, feature_ids, labels, cross_v, cross_u, cross_bias, w_in, b_in, w_out):
    warm_slots = N_MEMBER * WCAP
    slot_total = H + warm_slots + N_GROUP * CCAP
    warm_base = (jnp.arange(N_MEMBER, dtype=jnp.int32) * WDEV)[:, None]
    cold_base = (jnp.arange(N_GROUP, dtype=jnp.int32) * CDEV)[:, None]

    def per_device(carry, device):
        hot_acc, warm_acc, cold_acc = carry
        group_id = device // N_MEMBER
        lane_id = device % N_MEMBER
        warm_index = (warm_serve[group_id, :, lane_id, :] + warm_base).reshape(-1).astype(jnp.int32)
        cold_index = (cold_serve[:, lane_id, group_id, :] + cold_base).reshape(-1).astype(jnp.int32)
        buffer = jnp.concatenate([hot_table, warm_table[warm_index], cold_table[cold_index]], axis=0)
        start = (device * B_DEV).astype(jnp.int32)
        row_ids = lax.dynamic_slice_in_dim(feature_ids, start, B_DEV, 0)
        target = lax.dynamic_slice_in_dim(labels, start, B_DEV, 0).astype(jnp.float32)
        d_rows = sample_grads(buffer, row_ids, target, cross_v, cross_u, cross_bias, w_in, b_in, w_out)
        summed = jax.ops.segment_sum(d_rows, row_ids.reshape(-1), num_segments=slot_total)
        hot_acc = hot_acc + summed[:H]
        warm_acc = warm_acc.at[warm_index].add(summed[H:H + warm_slots])
        cold_acc = cold_acc.at[cold_index].add(summed[H + warm_slots:])
        return (hot_acc, warm_acc, cold_acc), None

    start_state = (jnp.zeros((H, E), jnp.float32), jnp.zeros((WDEV * N_MEMBER, E), jnp.float32), jnp.zeros((CDEV * N_GROUP, E), jnp.float32))
    final_state, _ = lax.scan(per_device, start_state, jnp.arange(N_GROUP * N_MEMBER, dtype=jnp.int32))
    return (final_state[0], final_state[1], final_state[2])
```

```python
import functools

import jax
import jax.numpy as jnp
from jax import lax
from jax.experimental import pallas as pl
from jax.experimental.pallas import tpu as pltpu
from jax.sharding import PartitionSpec as P

F32 = jnp.float32
BF16 = jnp.bfloat16
VMEM = pl.BlockSpec(memory_space=pltpu.VMEM)
ANY = pl.BlockSpec(memory_space=pl.ANY)
TILE = 256


def up(value, step):
    return (value + step - 1) // step * step


def iota(shape, axis):
    return lax.broadcasted_iota(jnp.int32, shape, axis)


def hits(left, right):
    return jnp.where(left == right, 1.0, 0.0).astype(BF16)


def dot(a, b):
    return jnp.dot(a, b, preferred_element_type=F32)


def dot_nt(a, b):
    return lax.dot_general(a, b, (((1,), (1,)), ((), ())), preferred_element_type=F32)


def column_of(row):
    size = row.shape[1]
    same = iota((size, size), 0) == iota((size, size), 1)
    return jnp.sum(jnp.where(same, row, 0), axis=1, keepdims=True)


def row_of(column):
    size = column.shape[0]
    same = iota((size, size), 0) == iota((size, size), 1)
    return jnp.sum(jnp.where(same, column, 0), axis=0, keepdims=True)


def tower_kernel(
    hot_ref, warm_ref, cold_ref, ids_ref, label_ref, bias_ref, b_in_ref, w_out_ref,
    v_hbm, u_hbm, w_hbm,
    member_ref, cold_out_ref,
    table, turned, inputs, crossed, d_layer, narrow, preact, total, v_ref, u_ref, w_ref, sems,
):
    copies = [
        pltpu.make_async_copy(v_hbm, v_ref, sems.at[0]),
        pltpu.make_async_copy(u_hbm, u_ref, sems.at[1]),
        pltpu.make_async_copy(w_hbm, w_ref, sems.at[2]),
    ]
    for copy in copies:
        copy.start()
    batch = ids_ref.shape[0]
    width = hot_ref.shape[1]
    fields = ids_ref.shape[1]
    steps = inputs.shape[1] // TILE
    each = TILE // width
    hot_rows = hot_ref.shape[0]
    warm_rows = warm_ref.shape[0]
    cold_rows = cold_ref.shape[0]
    slots = hot_rows + warm_rows + cold_rows
    table[0:hot_rows, :] = hot_ref[...]
    table[hot_rows : hot_rows + warm_rows, :] = warm_ref[...]
    table[hot_rows + warm_rows : slots, :] = cold_ref[...]

    def cols(step):
        return pl.ds(pl.multiple_of(step * TILE, TILE), TILE)

    narrow[...] = jnp.zeros_like(narrow)
    copies[0].wait()

    @pl.loop(0, steps)
    def _(step):
        pieces = []
        for k in range(each):
            field = step * each + k
            ids = jnp.sum(
                jnp.where(iota((batch, fields), 1) == field, ids_ref[...], 0), axis=1, keepdims=True
            )
            turned[pl.ds(field, 1), :] = row_of(ids)
            chosen = hits(iota((batch, slots), 1), ids)
            pieces.append(dot(chosen, table[...]).astype(BF16))
        part = jnp.concatenate(pieces, axis=1)
        inputs[:, cols(step)] = part
        narrow[...] += dot(part, v_ref[cols(step), :])

    low = narrow[...].astype(BF16)
    preact[...] = jnp.zeros_like(preact)
    copies[1].wait()
    copies[2].wait()

    @pl.loop(0, steps)
    def _(step):
        part = inputs[:, cols(step)].astype(F32)
        cross = dot(low, u_ref[:, cols(step)]) + bias_ref[:, cols(step)]
        crossed[:, cols(step)] = cross
        layer_one = (part * cross + part).astype(BF16)
        preact[...] += dot(layer_one, w_ref[cols(step), :])

    pre = preact[...] + b_in_ref[...]
    gate = jax.nn.sigmoid(pre)
    w_out = w_out_ref[...].astype(F32)
    hidden = (pre * gate).astype(BF16).astype(F32)
    logits = jnp.sum(hidden * w_out, axis=1, keepdims=True)
    d_logit = jax.nn.sigmoid(logits) - column_of(label_ref[...].astype(F32))
    d_hidden = (d_logit * w_out * gate * (1.0 + pre * (1.0 - gate))).astype(BF16)
    narrow[...] = jnp.zeros_like(narrow)

    @pl.loop(0, steps)
    def _(step):
        part = inputs[:, cols(step)].astype(F32)
        d_part = dot_nt(d_hidden, w_ref[cols(step), :])
        d_layer[:, cols(step)] = d_part
        d_crossed = (d_part * part).astype(BF16)
        narrow[...] += dot_nt(d_crossed, u_ref[:, cols(step)])

    d_low = narrow[...].astype(BF16)
    total[...] = jnp.zeros_like(total)

    @pl.loop(0, steps)
    def _(step):
        d_in = d_layer[:, cols(step)] * (crossed[:, cols(step)] + 1.0)
        d_in += dot_nt(d_low, v_ref[cols(step), :])
        high = d_in.astype(BF16)
        rest = (d_in - high.astype(F32)).astype(BF16)
        places, values = [], []
        for k in range(each):
            ids = turned[pl.ds(step * each + k, 1), :]
            places.append(hits(iota((slots, batch), 0), ids))
            piece = slice(k * width, (k + 1) * width)
            values.append(jnp.concatenate([high[:, piece], rest[:, piece]], axis=1))
        total[...] += dot(jnp.concatenate(places, axis=1), jnp.concatenate(values, axis=0))

    members = member_ref.shape[0]
    hot_each = hot_rows // members
    warm_each = warm_rows // members

    def rows(start, size):
        return (total[start : start + size, :width] + total[start : start + size, width:]).astype(BF16)

    for m in range(members):
        member_ref[m, 0:hot_each, :] = rows(m * hot_each, hot_each)
        member_ref[m, hot_each : hot_each + warm_each, :] = rows(hot_rows + m * warm_each, warm_each)
    cold_out_ref[...] = rows(hot_rows + warm_rows, cold_rows)


def tower(hot, warm, cold, ids, labels, bias, b_in, w_out, v, u, w, members):
    batch, fields = ids.shape
    width = hot.shape[1]
    wide, rank = v.shape
    hid = w.shape[1]
    slots = hot.shape[0] + warm.shape[0] + cold.shape[0]
    each = (hot.shape[0] + warm.shape[0]) // members
    flops = 2 * batch * wide * (2 * rank + hid) * 2 + 4 * batch * fields * slots * width * 2
    return pl.pallas_call(
        tower_kernel,
        name="tower",
        out_shape=(
            jax.ShapeDtypeStruct((members, each, width), BF16),
            jax.ShapeDtypeStruct(cold.shape, BF16),
        ),
        in_specs=[VMEM] * 8 + [ANY] * 3,
        out_specs=(VMEM, VMEM),
        scratch_shapes=[
            pltpu.VMEM((slots, width), BF16),
            pltpu.VMEM((up(fields, 8), batch), jnp.int32),
            pltpu.VMEM((batch, wide), BF16),
            pltpu.VMEM((batch, wide), F32),
            pltpu.VMEM((batch, wide), F32),
            pltpu.VMEM((batch, rank), F32),
            pltpu.VMEM((batch, hid), F32),
            pltpu.VMEM((slots, 2 * width), F32),
            pltpu.VMEM(v.shape, BF16),
            pltpu.VMEM(u.shape, BF16),
            pltpu.VMEM(w.shape, BF16),
            pltpu.SemaphoreType.DMA((3,)),
        ],
        compiler_params=pltpu.CompilerParams(vmem_limit_bytes=40 * 2**20),
        cost_estimate=pl.CostEstimate(flops=flops, bytes_accessed=10_000_000, transcendentals=batch * hid),
    )(hot, warm, cold, ids, labels, bias, b_in, w_out, v, u, w)


def call(kernel, name, out_shape, args, flops):
    single = isinstance(out_shape, jax.ShapeDtypeStruct)
    return pl.pallas_call(
        kernel,
        name=name,
        out_shape=out_shape,
        in_specs=[VMEM] * len(args),
        out_specs=VMEM if single else tuple(VMEM for _ in out_shape),
        compiler_params=pltpu.CompilerParams(vmem_limit_bytes=32 * 2**20),
        cost_estimate=pl.CostEstimate(flops=flops, bytes_accessed=2_000_000, transcendentals=0),
    )(*args)


def owner_kernel(chunk, slot, groups, keep, got_ref, cold_ref, to_ref, out_ref):
    out_rows = groups * slot
    place = iota((out_rows, 1), 0)
    group, at = place // slot, place % slot
    keeps = keep // groups
    wanted = jnp.where(at < chunk, group * chunk + at, -1)
    cold_wanted = jnp.where((at >= chunk) & (at < chunk + keeps), group * keeps + at - chunk, -1)
    out = dot(hits(wanted, to_ref[...]), got_ref[...])
    out += dot(hits(cold_wanted, iota((out_rows, keep), 1)), cold_ref[...])
    out_ref[...] = out.astype(BF16)


def finish_kernel(chunk, keeps, got_ref, chunk_ref, cold_ref):
    groups, slot, width = got_ref.shape
    summed = jnp.sum(got_ref[...].astype(F32), axis=0)
    chunk_ref[...] = jnp.broadcast_to(summed.astype(BF16)[None], chunk_ref.shape)
    cold_rows = cold_ref.shape[0]
    place = iota((cold_rows, 1), 0)
    wanted = place // keeps * slot + chunk + place % keeps
    flat = got_ref[...].reshape(groups * slot, width)
    cold_ref[...] = dot(hits(wanted, iota((cold_rows, groups * slot), 1)), flat).astype(BF16)


def spread_kernel(chunk, got_ref, cold_ref, warm_ref, out_ref):
    groups, slot, width = got_ref.shape
    members = out_ref.shape[0]
    warm_rows = warm_ref.shape[0]
    cold_rows = cold_ref.shape[0]
    hot_each = out_ref.shape[1] - cold_rows
    flat = got_ref[...].reshape(groups * slot, width)

    def pick(start, rows):
        place = iota((rows, 1), 0) + start
        wanted = place // chunk * slot + place % chunk
        return dot(hits(wanted, iota((rows, groups * slot), 1)), flat)

    warm_ref[...] = pick(0, warm_rows)
    hot = pick(warm_rows, hot_each).astype(BF16)
    for m in range(members):
        out_ref[m, 0:hot_each, :] = hot
        out_ref[m, hot_each : hot_each + cold_rows, :] = cold_ref[...]


def last_kernel(got_ref, to_ref, hot_ref, cold_ref):
    members, each, width = got_ref.shape
    hot_each = hot_ref.shape[0] // members
    cold_local = cold_ref.shape[0]
    rows = []
    for m in range(members):
        hot_ref[m * hot_each : (m + 1) * hot_each, :] = got_ref[m, 0:hot_each, :].astype(F32)
        rows.append(got_ref[m, hot_each:each, :])
    flat = jnp.concatenate(rows, axis=0)
    cold_ref[...] = dot(hits(iota((cold_local, flat.shape[0]), 0), to_ref[...]), flat)


def per_device(
    hot_table, warm_table, cold_table, warm_serve, cold_serve, feature_ids, labels,
    cross_v, cross_u, cross_bias, w_in, b_in, w_out,
):
    width = hot_table.shape[1]
    hot_rows = hot_table.shape[0]
    warm_local = warm_table.shape[0]
    cold_local = cold_table.shape[0]
    warm_list = warm_serve[0, 0]
    cold_list = cold_serve[0, 0]
    members, wcap = warm_list.shape
    groups, ccap = cold_list.shape
    warm_slots = members * wcap
    cold_slots = groups * ccap
    hot_each = hot_rows // members
    chunk = up(warm_local + hot_each, groups) // groups
    slot = up(chunk + ccap, 16)

    def exchange(x, axis):
        return lax.all_to_all(x, axis, split_axis=0, concat_axis=0, tiled=True)

    cold_to = lax.all_gather(cold_list.reshape(1, cold_slots), "member", axis=1, tiled=True)
    warm_wanted = warm_table[warm_list.reshape(-1)].reshape(members, wcap, width)
    warm_fetched = exchange(warm_wanted, "member").reshape(warm_slots, width)
    cold_wanted = cold_table[cold_list.reshape(-1)].reshape(groups, ccap, width)
    cold_fetched = exchange(cold_wanted, "group").reshape(cold_slots, width)

    to_members, cold_part = tower(
        hot_table, warm_fetched, cold_fetched, feature_ids, labels.reshape(1, -1),
        cross_bias.reshape(1, -1), b_in.reshape(1, -1), w_out.reshape(1, -1),
        cross_v, cross_u, w_in, members,
    )
    got = exchange(to_members, "member")

    hot_to = jnp.broadcast_to(warm_local + jnp.arange(hot_each, dtype=jnp.int32)[None], (members, hot_each))
    row_to = jnp.concatenate([hot_to, warm_list], axis=1).reshape(1, -1)
    to_groups = call(
        functools.partial(owner_kernel, chunk, slot, groups, cold_slots),
        "owner",
        jax.ShapeDtypeStruct((groups * slot, width), BF16),
        (got.reshape(-1, width), cold_part, row_to),
        2 * groups * slot * width * (row_to.shape[1] + cold_slots),
    )
    summands = exchange(to_groups.reshape(groups, slot, width), "group")
    my_chunk, my_cold = call(
        functools.partial(finish_kernel, chunk, ccap),
        "finish",
        (
            jax.ShapeDtypeStruct((groups, slot, width), BF16),
            jax.ShapeDtypeStruct((cold_slots, width), BF16),
        ),
        (summands,),
        2 * groups * slot * width * cold_slots,
    )
    chunks = exchange(my_chunk, "group")
    warm_grad, to_all = call(
        functools.partial(spread_kernel, chunk),
        "spread",
        (
            jax.ShapeDtypeStruct((warm_local, width), F32),
            jax.ShapeDtypeStruct((members, hot_each + cold_slots, width), BF16),
        ),
        (chunks, my_cold),
        2 * groups * slot * width * (warm_local + hot_each),
    )
    last = exchange(to_all, "member")
    hot_grad, cold_grad = call(
        last_kernel,
        "last",
        (
            jax.ShapeDtypeStruct((hot_rows, width), F32),
            jax.ShapeDtypeStruct((cold_local, width), F32),
        ),
        (last, cold_to),
        2 * cold_local * members * cold_slots * width,
    )
    return hot_grad, warm_grad, cold_grad


def solution(mesh):
    placed = (
        P(),
        P("member", None),
        P("group", None),
        P("group", "member", None, None),
        P("group", "member", None, None),
        P(("group", "member"), None),
        P(("group", "member")),
        P(),
        P(),
        P(),
        P(),
        P(),
        P(),
    )
    return jax.shard_map(
        per_device,
        mesh=mesh,
        in_specs=placed,
        out_specs=(P(), P("member", None), P("group", None)),
        check_vma=False,
    )
```

```python
import functools

import jax
import jax.numpy as jnp
from jax import lax
from jax.experimental import pallas as pl
from jax.experimental.pallas import tpu as pltpu
from jax.sharding import PartitionSpec as P

F32 = jnp.float32
BF16 = jnp.bfloat16
VMEM = pl.BlockSpec(memory_space=pltpu.VMEM)
HBM = pl.BlockSpec(memory_space=pltpu.HBM)
TILE = 512
LANES = 128
EXTRA = 16


def up(value, step):
    return (value + step - 1) // step * step


def iota(shape, axis):
    return lax.broadcasted_iota(jnp.int32, shape, axis)


def hits(left, right):
    return jnp.where(left == right, 1.0, 0.0).astype(BF16)


def short_hits(left, right):
    met = left.astype(jnp.int16) == right.astype(jnp.int16)
    return jnp.where(met, jnp.ones((), BF16), jnp.zeros((), BF16))


def dot(a, b):
    return jnp.dot(a, b, preferred_element_type=F32)


def dot_nt(a, b):
    return lax.dot_general(a, b, (((1,), (1,)), ((), ())), preferred_element_type=F32)


def column_of(row):
    size = row.shape[1]
    same = iota((size, size), 0) == iota((size, size), 1)
    return jnp.sum(jnp.where(same, row, 0), axis=1, keepdims=True)


def standing(ids_ref):
    fields, batch = ids_ref.shape
    filled = jnp.concatenate([ids_ref[...], jnp.zeros((LANES - fields, batch), jnp.int32)], axis=0)
    return filled.T


def field_column(stood, field):
    return jnp.sum(jnp.where(iota(stood.shape, 1) == field, stood, 0), axis=1, keepdims=True)


def columns(step):
    return pl.ds(pl.multiple_of(step * TILE, TILE), TILE)


def lookup_kernel(hot_ref, warm_ref, ids_ref, out_ref, table, stood_ref):
    rows, width = table.shape
    hot_rows = hot_ref.shape[0]
    table[0:hot_rows, :] = hot_ref[...]
    table[hot_rows:, :] = warm_ref[...]
    batch = ids_ref.shape[1]
    stood_ref[...] = standing(ids_ref)

    @pl.loop(0, out_ref.shape[1] // TILE, unroll=True)
    def _(step):
        pieces = []
        for k in range(TILE // width):
            ids = field_column(stood_ref[...], step * (TILE // width) + k)
            chosen = short_hits(iota((batch, rows), 1), ids)
            pieces.append(dot(chosen, table[...]).astype(BF16))
        out_ref[:, columns(step)] = jnp.concatenate(pieces, axis=1)


def tower_kernel(
    hot_rows, warm_rows,
    found_ref, cold_ref, ids_ref, label_ref, bias_ref, b_in_ref, w_out_ref, v_ref, u_hbm, w_hbm,
    member_ref, cold_out_ref,
    stood_ref, inputs, crossed, d_layer, narrow, preact, total, u_ref, w_ref, sems,
):
    copies = [pltpu.make_async_copy(u_hbm, u_ref, sems.at[0]), pltpu.make_async_copy(w_hbm, w_ref, sems.at[1])]
    for copy in copies:
        copy.start()
    fields, batch = ids_ref.shape
    width = cold_ref.shape[1]
    steps = inputs.shape[1] // TILE
    each = TILE // width
    cold_rows = cold_ref.shape[0]
    slots = hot_rows + warm_rows + cold_rows
    stood_ref[...] = standing(ids_ref)
    narrow[...] = jnp.zeros_like(narrow)

    @pl.loop(0, steps, unroll=True)
    def _(step):
        pieces = []
        for k in range(each):
            ids = field_column(stood_ref[...], step * each + k)
            chosen = short_hits(iota((batch, cold_rows), 1) + (slots - cold_rows), ids)
            pieces.append(dot(chosen, cold_ref[...]))
        fetched = jnp.concatenate(pieces, axis=1)
        part = (found_ref[:, columns(step)].astype(F32) + fetched).astype(BF16)
        inputs[:, columns(step)] = part
        narrow[...] += dot(part, v_ref[columns(step), :])

    low = narrow[...].astype(BF16)
    preact[...] = jnp.zeros_like(preact)
    for copy in copies:
        copy.wait()

    @pl.loop(0, steps, unroll=True)
    def _(step):
        part = inputs[:, columns(step)].astype(F32)
        cross = dot(low, u_ref[:, columns(step)]) + bias_ref[:, columns(step)]
        crossed[:, columns(step)] = cross
        layer_one = (part * cross + part).astype(BF16)
        preact[...] += dot(layer_one, w_ref[columns(step), :])

    pre = preact[...] + b_in_ref[...]
    gate = jax.nn.sigmoid(pre)
    w_out = w_out_ref[...].astype(F32)
    hidden = (pre * gate).astype(BF16).astype(F32)
    logits = jnp.sum(hidden * w_out, axis=1, keepdims=True)
    d_logit = jax.nn.sigmoid(logits) - column_of(label_ref[...].astype(F32))
    d_hidden = (d_logit * w_out * gate * (1.0 + pre * (1.0 - gate))).astype(BF16)
    narrow[...] = jnp.zeros_like(narrow)

    @pl.loop(0, steps, unroll=True)
    def _(step):
        part = inputs[:, columns(step)].astype(F32)
        d_part = dot_nt(d_hidden, w_ref[columns(step), :])
        d_layer[:, columns(step)] = d_part
        d_crossed = (d_part * part).astype(BF16)
        narrow[...] += dot_nt(d_crossed, u_ref[:, columns(step)])

    d_low = narrow[...].astype(BF16)
    total[...] = jnp.zeros_like(total)

    @pl.loop(0, steps, unroll=True)
    def _(step):
        d_in = d_layer[:, columns(step)] * (crossed[:, columns(step)] + 1.0)
        d_in += dot_nt(d_low, v_ref[columns(step), :])
        high = d_in.astype(BF16)
        rest = (d_in - high.astype(F32)).astype(BF16)
        places, values = [], []
        for k in range(each):
            ids = ids_ref[pl.ds(step * each + k, 1), :]
            places.append(short_hits(iota((slots, batch), 0), ids))
            piece = slice(k * width, (k + 1) * width)
            values.append(jnp.concatenate([high[:, piece], rest[:, piece]], axis=1))
        total[...] += dot(jnp.concatenate(places, axis=1), jnp.concatenate(values, axis=0))

    members = member_ref.shape[0]
    hot_each = hot_rows // members
    warm_each = warm_rows // members

    def rows(start, size):
        return (total[start : start + size, :width] + total[start : start + size, width:]).astype(BF16)

    for m in range(members):
        member_ref[m, 0:hot_each, :] = rows(m * hot_each, hot_each)
        member_ref[m, hot_each : hot_each + warm_each, :] = rows(hot_rows + m * warm_each, warm_each)
    cold_out_ref[...] = rows(hot_rows + warm_rows, cold_rows)


def call(kernel, name, out_shape, args, flops, scratch=(), vmem=8, transcendentals=0, apart=0):
    single = isinstance(out_shape, jax.ShapeDtypeStruct)
    return pl.pallas_call(
        kernel,
        name=name,
        out_shape=out_shape,
        in_specs=[VMEM] * (len(args) - apart) + [HBM] * apart,
        out_specs=VMEM if single else tuple(VMEM for _ in out_shape),
        scratch_shapes=list(scratch),
        compiler_params=pltpu.CompilerParams(vmem_limit_bytes=vmem * 2**20),
        cost_estimate=pl.CostEstimate(flops=flops, bytes_accessed=2_000_000, transcendentals=transcendentals),
    )(*args)


def lookup(hot, warm, ids):
    fields, batch = ids.shape
    width = hot.shape[1]
    rows = hot.shape[0] + warm.shape[0]
    return call(
        lookup_kernel, "lookup", jax.ShapeDtypeStruct((batch, fields * width), BF16), (hot, warm, ids),
        4 * batch * fields * rows * width,
        [pltpu.VMEM((rows, width), BF16), pltpu.VMEM((batch, LANES), jnp.int32)], 16,
    )


def tower(found, cold, ids, labels, bias, b_in, w_out, v, u, w, hot_rows, warm_rows, members):
    fields, batch = ids.shape
    width = cold.shape[1]
    wide, rank = v.shape
    hid = w.shape[1]
    slots = hot_rows + warm_rows + cold.shape[0]
    each = (hot_rows + warm_rows) // members
    flops = 2 * batch * wide * (2 * rank + hid) * 2 + 4 * batch * fields * slots * width * 2
    return call(
        functools.partial(tower_kernel, hot_rows, warm_rows),
        "tower",
        (
            jax.ShapeDtypeStruct((members, each, width), BF16),
            jax.ShapeDtypeStruct(cold.shape, BF16),
        ),
        (found, cold, ids, labels, bias, b_in, w_out, v, u, w),
        flops,
        [
            pltpu.VMEM((batch, LANES), jnp.int32),
            pltpu.VMEM((batch, wide), BF16),
            pltpu.VMEM((batch, wide), F32),
            pltpu.VMEM((batch, wide), F32),
            pltpu.VMEM((batch, rank), F32),
            pltpu.VMEM((batch, hid), F32),
            pltpu.VMEM((slots, 2 * width), F32),
            pltpu.VMEM(u.shape, BF16),
            pltpu.VMEM(w.shape, BF16),
            pltpu.SemaphoreType.DMA((2,)),
        ],
        52,
        batch * hid,
        2,
    )


def serve_cold_kernel(table_ref, list_ref, out_ref):
    ccap, groups = list_ref.shape
    shape = (out_ref.shape[0], groups)
    row, group = iota(shape, 0), iota(shape, 1)
    ids = jnp.zeros(shape, jnp.int32)
    for k in range(ccap):
        ids = jnp.where((row // ccap == group) & (row % ccap == k), list_ref[k : k + 1, :], ids)
    ids = jnp.sum(ids, axis=1, keepdims=True)
    out_ref[...] = dot(short_hits(iota((shape[0], table_ref.shape[0]), 1), ids), table_ref[...]).astype(BF16)


def serve_warm_kernel(table_ref, list_ref, out_ref):
    members, wcap = list_ref.shape
    for m in range(members):
        ids = column_of(list_ref[m : m + 1, :])
        out_ref[m] = dot(short_hits(iota((wcap, table_ref.shape[0]), 1), ids), table_ref[...]).astype(BF16)


def owner_kernel(warm_local, chunk, slot, groups, got_ref, cold_ref, list_ref, out_ref):
    out_rows = groups * slot
    members = list_ref.shape[0]
    keep = cold_ref.shape[0]
    keeps = keep // groups
    hot_each = got_ref.shape[0] // members - list_ref.shape[1]
    hot_to = warm_local + iota((1, hot_each), 1)
    to = jnp.concatenate([piece for m in range(members) for piece in (hot_to, list_ref[m : m + 1, :])], axis=1)
    place = iota((out_rows, 1), 0)
    group, at = place // slot, place % slot
    wanted = jnp.where(at < chunk, group * chunk + at, -1)
    cold_wanted = jnp.where((at >= chunk) & (at < chunk + keeps), group * keeps + at - chunk, -1)
    out = dot(hits(wanted, to), got_ref[...])
    out += dot(hits(cold_wanted, iota((out_rows, keep), 1)), cold_ref[...])
    out_ref[...] = out.astype(BF16)


def finish_kernel(chunk, slot, keeps, got_ref, chunk_ref, cold_ref):
    total_rows = got_ref.shape[0]
    groups = total_rows // slot
    rows = up(chunk, 16)
    shape = (rows, total_rows)
    own = jnp.where(iota(shape, 0) < chunk, iota(shape, 0), -1)
    summed = dot(hits(own, iota(shape, 1) % slot), got_ref[...]).astype(BF16)
    place = iota((groups * chunk, rows), 0) % chunk
    chunk_ref[...] = dot(hits(place, iota((groups * chunk, rows), 1)), summed).astype(BF16)
    cold_rows = cold_ref.shape[0]
    row = iota((cold_rows, 1), 0)
    wanted = row % groups * slot + chunk + row // groups
    cold_ref[...] = dot(hits(wanted, iota((cold_rows, total_rows), 1)), got_ref[...]).astype(BF16)


def spread_kernel(got_ref, cold_ref, list_ref, warm_ref, out_ref):
    members = out_ref.shape[0]
    warm_rows, width = warm_ref.shape
    cold_rows = cold_ref.shape[0]
    ccap, groups = list_ref.shape
    hot_each = out_ref.shape[1] - cold_rows - EXTRA
    warm_ref[...] = got_ref[0:warm_rows, :].astype(F32)
    hot = got_ref[warm_rows : warm_rows + hot_each, :]
    places = list_ref[...]
    blank = jnp.zeros((EXTRA, groups), jnp.int32)
    row = iota((EXTRA, groups), 0)
    for k in range(ccap):
        blank = jnp.where(row == 2 * k, places[k : k + 1, :] // 32, blank)
        blank = jnp.where(row == 2 * k + 1, places[k : k + 1, :] % 32, blank)
    code = jnp.concatenate([blank.astype(F32), jnp.zeros((EXTRA, width - groups), F32)], axis=1).astype(BF16)
    for m in range(members):
        out_ref[m, 0:hot_each, :] = hot
        out_ref[m, hot_each : hot_each + cold_rows, :] = cold_ref[...]
        out_ref[m, hot_each + cold_rows :, :] = code


def last_kernel(groups, ccap, got_ref, hot_ref, cold_ref):
    members, each, width = got_ref.shape
    hot_each = hot_ref.shape[0] // members
    cold_local = cold_ref.shape[0]
    last_row = each - EXTRA
    total = jnp.zeros((cold_local, width), F32)
    for m in range(members):
        hot_ref[m * hot_each : (m + 1) * hot_each, :] = got_ref[m, 0:hot_each, :].astype(F32)
        code = got_ref[m, last_row:, :].astype(F32)
        to = [code[2 * k : 2 * k + 1, :groups] * 32.0 + code[2 * k + 1 : 2 * k + 2, :groups] for k in range(ccap)]
        to = jnp.concatenate(to, axis=1).astype(jnp.int32)
        total += dot(short_hits(iota((cold_local, to.shape[1]), 0), to), got_ref[m, hot_each:last_row, :])
    cold_ref[...] = total


def per_device(
    hot_table, warm_table, cold_table, warm_serve, cold_serve, feature_ids, labels,
    cross_v, cross_u, cross_bias, w_in, b_in, w_out,
):
    width = hot_table.shape[1]
    hot_rows = hot_table.shape[0]
    warm_local = warm_table.shape[0]
    cold_local = cold_table.shape[0]
    warm_list = warm_serve[0, 0]
    cold_list = cold_serve[0, 0].T
    ids = feature_ids.T
    members, wcap = warm_list.shape
    ccap, groups = cold_list.shape
    warm_slots = members * wcap
    cold_slots = groups * ccap
    hot_each = hot_rows // members
    chunk = up(up(warm_local + hot_each, groups) // groups, 4)
    slot = up(chunk + ccap, 2)

    def exchange(x, axis):
        return lax.all_to_all(x, axis, split_axis=0, concat_axis=0, tiled=True)

    def exchange_rows(x, tile):
        parts = x.reshape(x.shape[0] // tile, tile, width)
        return exchange(parts, "group").reshape(x.shape)

    def shape(*dims, kind=BF16):
        return jax.ShapeDtypeStruct(dims, kind)

    cold_wanted = call(
        serve_cold_kernel, "serve_cold", shape(cold_slots, width), (cold_table, cold_list),
        2 * cold_slots * cold_local * width,
    )
    cold_fetched = exchange_rows(cold_wanted, ccap)
    warm_wanted = call(
        serve_warm_kernel, "serve_warm", shape(members, wcap, width), (warm_table, warm_list),
        2 * warm_slots * warm_local * width,
    )
    warm_fetched = exchange(warm_wanted, "member").reshape(warm_slots, width)
    found = lookup(hot_table, warm_fetched, ids)
    to_members, cold_part = tower(
        found, cold_fetched, ids, labels.reshape(1, -1),
        cross_bias.reshape(1, -1), b_in.reshape(1, -1), w_out.reshape(1, -1),
        cross_v, cross_u, w_in, hot_rows, warm_slots, members,
    )
    got = exchange(to_members, "member")
    to_groups = call(
        functools.partial(owner_kernel, warm_local, chunk, slot, groups),
        "owner",
        shape(groups * slot, width),
        (got.reshape(-1, width), cold_part, warm_list),
        2 * groups * slot * width * (hot_rows + warm_slots + cold_slots),
        vmem=16,
    )
    summands = exchange_rows(to_groups, 2)
    my_chunk, my_cold = call(
        functools.partial(finish_kernel, chunk, slot, ccap),
        "finish",
        (shape(groups * chunk, width), shape(cold_slots, width)),
        (summands,),
        2 * groups * slot * width * cold_slots,
    )
    chunks = exchange_rows(my_chunk, 4)
    warm_grad, to_all = call(
        spread_kernel,
        "spread",
        (shape(warm_local, width, kind=F32), shape(members, hot_each + cold_slots + EXTRA, width)),
        (chunks, my_cold, cold_list),
        2 * groups * slot * width,
    )
    last = exchange(to_all, "member")
    hot_grad, cold_grad = call(
        functools.partial(last_kernel, groups, ccap),
        "last",
        (shape(hot_rows, width, kind=F32), shape(cold_local, width, kind=F32)),
        (last,),
        2 * cold_local * members * cold_slots * width,
    )
    return hot_grad, warm_grad, cold_grad


def solution(mesh):
    placed = (
        P(),
        P("member", None),
        P("group", None),
        P("group", "member", None, None),
        P("group", "member", None, None),
        P(("group", "member"), None),
        P(("group", "member")),
        P(),
        P(),
        P(),
        P(),
        P(),
        P(),
    )
    return jax.shard_map(
        per_device,
        mesh=mesh,
        in_specs=placed,
        out_specs=(P(), P("member", None), P("group", None)),
        check_vma=False,
    )
```

```python
import functools

import jax
import jax.numpy as jnp
from jax import lax
from jax.experimental import pallas as pl
from jax.experimental.pallas import tpu as pltpu
from jax.sharding import PartitionSpec as P

F32 = jnp.float32
BF16 = jnp.bfloat16
VMEM = pl.BlockSpec(memory_space=pltpu.VMEM)
HBM = pl.BlockSpec(memory_space=pltpu.HBM)
TILE = 512
LANES = 128
EXTRA = 16


def up(value, step):
    return (value + step - 1) // step * step


def iota(shape, axis):
    return lax.broadcasted_iota(jnp.int32, shape, axis)


def hits(left, right):
    return jnp.where(left == right, 1.0, 0.0).astype(BF16)


def short_hits(left, right):
    met = left.astype(jnp.int16) == right.astype(jnp.int16)
    return jnp.where(met, jnp.ones((), BF16), jnp.zeros((), BF16))


def dot(a, b):
    return jnp.dot(a, b, preferred_element_type=F32)


def dot_nt(a, b):
    return lax.dot_general(a, b, (((1,), (1,)), ((), ())), preferred_element_type=F32)


def column_of(row):
    size = row.shape[1]
    same = iota((size, size), 0) == iota((size, size), 1)
    return jnp.sum(jnp.where(same, row, 0), axis=1, keepdims=True)


def standing(ids_ref):
    fields, batch = ids_ref.shape
    filled = jnp.concatenate([ids_ref[...], jnp.zeros((LANES - fields, batch), jnp.int32)], axis=0)
    return filled.T


def field_column(stood, field):
    return jnp.sum(jnp.where(iota(stood.shape, 1) == field, stood, 0), axis=1, keepdims=True)


def columns(step):
    return pl.ds(step * TILE if isinstance(step, int) else pl.multiple_of(step * TILE, TILE), TILE)


def lookup_kernel(hot_ref, warm_ref, ids_ref, out_ref, table, stood_ref):
    rows, width = table.shape
    hot_rows = hot_ref.shape[0]
    table[0:hot_rows, :] = hot_ref[...]
    table[hot_rows:, :] = warm_ref[...]
    batch = ids_ref.shape[1]
    stood_ref[...] = standing(ids_ref)

    @pl.loop(0, out_ref.shape[1] // TILE, unroll=True)
    def _(step):
        pieces = []
        for k in range(TILE // width):
            ids = field_column(stood_ref[...], step * (TILE // width) + k)
            chosen = short_hits(iota((batch, rows), 1), ids)
            pieces.append(dot(chosen, table[...]).astype(BF16))
        out_ref[:, columns(step)] = jnp.concatenate(pieces, axis=1)


def tower_kernel(
    hot_rows, warm_rows,
    found_ref, cold_ref, ids_ref, label_ref, bias_ref, b_in_ref, w_out_ref, v_hbm, u_hbm, w_hbm,
    member_ref, cold_out_ref,
    stood_ref, inputs, crossed, d_layer, narrow, preact, total, v_ref, u_ref, w_ref, sems,
):
    v_copy = pltpu.make_async_copy(v_hbm, v_ref, sems.at[0])
    u_copy = pltpu.make_async_copy(u_hbm, u_ref, sems.at[1])
    w_copies = [
        pltpu.make_async_copy(w_hbm.at[pl.ds(at, TILE), :], w_ref.at[pl.ds(at, TILE), :], sems.at[2 + at // TILE])
        for at in range(0, w_ref.shape[0], TILE)
    ]
    for copy in (v_copy, u_copy, *w_copies):
        copy.start()
    fields, batch = ids_ref.shape
    width = cold_ref.shape[1]
    steps = inputs.shape[1] // TILE
    each = TILE // width
    cold_rows = cold_ref.shape[0]
    slots = hot_rows + warm_rows + cold_rows
    stood_ref[...] = standing(ids_ref)
    narrow[...] = jnp.zeros_like(narrow)
    v_copy.wait()

    @pl.loop(0, steps, unroll=True)
    def _(step):
        pieces = []
        for k in range(each):
            ids = field_column(stood_ref[...], step * each + k)
            chosen = short_hits(iota((batch, cold_rows), 1) + (slots - cold_rows), ids)
            pieces.append(dot(chosen, cold_ref[...]))
        fetched = jnp.concatenate(pieces, axis=1)
        part = (found_ref[:, columns(step)].astype(F32) + fetched).astype(BF16)
        inputs[:, columns(step)] = part
        narrow[...] += dot(part, v_ref[columns(step), :])

    low = narrow[...].astype(BF16)
    preact[...] = jnp.zeros_like(preact)
    u_copy.wait()

    for step in range(steps):
        w_copies[step].wait()
        part = inputs[:, columns(step)].astype(F32)
        cross = dot(low, u_ref[:, columns(step)]) + bias_ref[:, columns(step)]
        crossed[:, columns(step)] = cross
        layer_one = (part * cross + part).astype(BF16)
        preact[...] += dot(layer_one, w_ref[columns(step), :])

    pre = preact[...] + b_in_ref[...]
    gate = jax.nn.sigmoid(pre)
    w_out = w_out_ref[...].astype(F32)
    hidden = (pre * gate).astype(BF16).astype(F32)
    logits = jnp.sum(hidden * w_out, axis=1, keepdims=True)
    d_logit = jax.nn.sigmoid(logits) - column_of(label_ref[...].astype(F32))
    d_hidden = (d_logit * w_out * gate * (1.0 + pre * (1.0 - gate))).astype(BF16)
    narrow[...] = jnp.zeros_like(narrow)

    @pl.loop(0, steps, unroll=True)
    def _(step):
        part = inputs[:, columns(step)].astype(F32)
        d_part = dot_nt(d_hidden, w_ref[columns(step), :])
        d_layer[:, columns(step)] = d_part
        d_crossed = (d_part * part).astype(BF16)
        narrow[...] += dot_nt(d_crossed, u_ref[:, columns(step)])

    d_low = narrow[...].astype(BF16)
    total[...] = jnp.zeros_like(total)

    @pl.loop(0, steps, unroll=True)
    def _(step):
        d_in = d_layer[:, columns(step)] * (crossed[:, columns(step)] + 1.0)
        d_in += dot_nt(d_low, v_ref[columns(step), :])
        high = d_in.astype(BF16)
        for k in range(each):
            ids = field_column(stood_ref[...], step * each + k)
            piece = slice(k * width, (k + 1) * width)
            value = high[:, piece]
            total[...] += lax.dot_general(value, short_hits(iota((batch, slots), 1), ids), (((0,), (0,)), ((), ())), preferred_element_type=F32)

    members = member_ref.shape[0]
    hot_each = hot_rows // members
    warm_each = warm_rows // members

    turned = total[...].T

    def rows(start, size):
        return turned[start : start + size, :].astype(BF16)

    for m in range(members):
        member_ref[m, 0:hot_each, :] = rows(m * hot_each, hot_each)
        member_ref[m, hot_each : hot_each + warm_each, :] = rows(hot_rows + m * warm_each, warm_each)
    cold_out_ref[...] = rows(hot_rows + warm_rows, cold_rows)


def call(kernel, name, out_shape, args, flops, scratch=(), vmem=8, transcendentals=0, apart=0):
    single = isinstance(out_shape, jax.ShapeDtypeStruct)
    return pl.pallas_call(
        kernel,
        name=name,
        out_shape=out_shape,
        in_specs=[VMEM] * (len(args) - apart) + [HBM] * apart,
        out_specs=VMEM if single else tuple(VMEM for _ in out_shape),
        scratch_shapes=list(scratch),
        compiler_params=pltpu.CompilerParams(vmem_limit_bytes=vmem * 2**20),
        cost_estimate=pl.CostEstimate(flops=flops, bytes_accessed=2_000_000, transcendentals=transcendentals),
    )(*args)


def lookup(hot, warm, ids):
    fields, batch = ids.shape
    width = hot.shape[1]
    rows = hot.shape[0] + warm.shape[0]
    return call(
        lookup_kernel, "lookup", jax.ShapeDtypeStruct((batch, fields * width), BF16), (hot, warm, ids),
        4 * batch * fields * rows * width,
        [pltpu.VMEM((rows, width), BF16), pltpu.VMEM((batch, LANES), jnp.int32)], 16,
    )


def tower(found, cold, ids, labels, bias, b_in, w_out, v, u, w, hot_rows, warm_rows, members):
    fields, batch = ids.shape
    width = cold.shape[1]
    wide, rank = v.shape
    hid = w.shape[1]
    slots = hot_rows + warm_rows + cold.shape[0]
    each = (hot_rows + warm_rows) // members
    flops = 2 * batch * wide * (2 * rank + hid) * 2 + 4 * batch * fields * slots * width * 2
    return call(
        functools.partial(tower_kernel, hot_rows, warm_rows),
        "tower",
        (
            jax.ShapeDtypeStruct((members, each, width), BF16),
            jax.ShapeDtypeStruct(cold.shape, BF16),
        ),
        (found, cold, ids, labels, bias, b_in, w_out, v, u, w),
        flops,
        [
            pltpu.VMEM((batch, LANES), jnp.int32),
            pltpu.VMEM((batch, wide), BF16),
            pltpu.VMEM((batch, wide), F32),
            pltpu.VMEM((batch, wide), F32),
            pltpu.VMEM((batch, rank), F32),
            pltpu.VMEM((batch, hid), F32),
            pltpu.VMEM((width, slots), F32),
            pltpu.VMEM(v.shape, BF16),
            pltpu.VMEM(u.shape, BF16),
            pltpu.VMEM(w.shape, BF16),
            pltpu.SemaphoreType.DMA((2 + wide // TILE,)),
        ],
        52,
        batch * hid,
        3,
    )


def serve_cold_kernel(table_ref, list_ref, out_ref):
    ccap, groups = list_ref.shape
    shape = (out_ref.shape[0], groups)
    row, group = iota(shape, 0), iota(shape, 1)
    ids = jnp.zeros(shape, jnp.int32)
    for k in range(ccap):
        ids = jnp.where((row // ccap == group) & (row % ccap == k), list_ref[k : k + 1, :], ids)
    ids = jnp.sum(ids, axis=1, keepdims=True)
    out_ref[...] = dot(short_hits(iota((shape[0], table_ref.shape[0]), 1), ids), table_ref[...]).astype(BF16)


def serve_warm_kernel(table_ref, list_ref, out_ref):
    members, wcap = list_ref.shape
    for m in range(members):
        ids = column_of(list_ref[m : m + 1, :])
        out_ref[m] = dot(short_hits(iota((wcap, table_ref.shape[0]), 1), ids), table_ref[...]).astype(BF16)


def owner_kernel(warm_local, chunk, slot, groups, got_ref, cold_ref, list_ref, out_ref):
    out_rows = groups * slot
    members = list_ref.shape[0]
    keep = cold_ref.shape[0]
    keeps = keep // groups
    hot_each = got_ref.shape[0] // members - list_ref.shape[1]
    hot_to = warm_local + iota((1, hot_each), 1)
    to = jnp.concatenate([piece for m in range(members) for piece in (hot_to, list_ref[m : m + 1, :])], axis=1)
    place = iota((out_rows, 1), 0)
    group, at = place // slot, place % slot
    wanted = jnp.where(at < chunk, group * chunk + at, -1)
    cold_wanted = jnp.where((at >= chunk) & (at < chunk + keeps), group * keeps + at - chunk, -1)
    out = dot(hits(wanted, to), got_ref[...])
    out += dot(hits(cold_wanted, iota((out_rows, keep), 1)), cold_ref[...])
    out_ref[...] = out.astype(BF16)


def finish_kernel(chunk, slot, keeps, got_ref, chunk_ref, cold_ref):
    total_rows = got_ref.shape[0]
    groups = total_rows // slot
    rows = up(chunk, 16)
    shape = (rows, total_rows)
    own = jnp.where(iota(shape, 0) < chunk, iota(shape, 0), -1)
    summed = dot(hits(own, iota(shape, 1) % slot), got_ref[...]).astype(BF16)
    place = iota((groups * chunk, rows), 0) % chunk
    chunk_ref[...] = dot(hits(place, iota((groups * chunk, rows), 1)), summed).astype(BF16)
    cold_rows = cold_ref.shape[0]
    row = iota((cold_rows, 1), 0)
    wanted = row % groups * slot + chunk + row // groups
    cold_ref[...] = dot(hits(wanted, iota((cold_rows, total_rows), 1)), got_ref[...]).astype(BF16)


def spread_kernel(got_ref, cold_ref, list_ref, warm_ref, out_ref):
    warm_rows, width = warm_ref.shape
    cold_rows = cold_ref.shape[0]
    ccap, groups = list_ref.shape
    hot_each = out_ref.shape[0] - cold_rows - EXTRA
    warm_ref[...] = got_ref[0:warm_rows, :].astype(F32)
    out_ref[0:hot_each, :] = got_ref[warm_rows : warm_rows + hot_each, :]
    out_ref[hot_each : hot_each + cold_rows, :] = cold_ref[...]
    places = list_ref[...]
    blank = jnp.zeros((EXTRA, groups), jnp.int32)
    row = iota((EXTRA, groups), 0)
    for k in range(ccap):
        blank = jnp.where(row == 2 * k, places[k : k + 1, :] // 32, blank)
        blank = jnp.where(row == 2 * k + 1, places[k : k + 1, :] % 32, blank)
    code = jnp.concatenate([blank.astype(F32), jnp.zeros((EXTRA, width - groups), F32)], axis=1).astype(BF16)
    out_ref[hot_each + cold_rows :, :] = code


def last_kernel(groups, ccap, got_ref, hot_ref, cold_ref):
    members, each, width = got_ref.shape
    hot_each = hot_ref.shape[0] // members
    cold_local = cold_ref.shape[0]
    last_row = each - EXTRA
    total = jnp.zeros((cold_local, width), F32)
    for m in range(members):
        hot_ref[m * hot_each : (m + 1) * hot_each, :] = got_ref[m, 0:hot_each, :].astype(F32)
        code = got_ref[m, last_row:, :].astype(F32)
        to = [code[2 * k : 2 * k + 1, :groups] * 32.0 + code[2 * k + 1 : 2 * k + 2, :groups] for k in range(ccap)]
        to = jnp.concatenate(to, axis=1).astype(jnp.int32)
        total += dot(short_hits(iota((cold_local, to.shape[1]), 0), to), got_ref[m, hot_each:last_row, :])
    cold_ref[...] = total


def per_device(
    hot_table, warm_table, cold_table, warm_serve, cold_serve, feature_ids, labels,
    cross_v, cross_u, cross_bias, w_in, b_in, w_out,
):
    width = hot_table.shape[1]
    hot_rows = hot_table.shape[0]
    warm_local = warm_table.shape[0]
    cold_local = cold_table.shape[0]
    warm_list = warm_serve[0, 0]
    cold_list = cold_serve[0, 0].T
    ids = feature_ids.T
    members, wcap = warm_list.shape
    ccap, groups = cold_list.shape
    warm_slots = members * wcap
    cold_slots = groups * ccap
    hot_each = hot_rows // members
    chunk = up(up(warm_local + hot_each, groups) // groups, 4)
    slot = up(chunk + ccap, 2)

    def exchange(x, axis):
        return lax.all_to_all(x, axis, split_axis=0, concat_axis=0, tiled=True)

    def exchange_rows(x, tile):
        parts = x.reshape(x.shape[0] // tile, tile, width)
        return exchange(parts, "group").reshape(x.shape)

    def shape(*dims, kind=BF16):
        return jax.ShapeDtypeStruct(dims, kind)

    cold_wanted = call(
        serve_cold_kernel, "serve_cold", shape(cold_slots, width), (cold_table, cold_list),
        2 * cold_slots * cold_local * width,
    )
    cold_fetched = exchange_rows(cold_wanted, ccap)
    warm_wanted = call(
        serve_warm_kernel, "serve_warm", shape(members, wcap, width), (warm_table, warm_list),
        2 * warm_slots * warm_local * width,
    )
    warm_fetched = exchange(warm_wanted, "member").reshape(warm_slots, width)
    found = lookup(hot_table, warm_fetched, ids)
    to_members, cold_part = tower(
        found, cold_fetched, ids, labels.reshape(1, -1),
        cross_bias.reshape(1, -1), b_in.reshape(1, -1), w_out.reshape(1, -1),
        cross_v, cross_u, w_in, hot_rows, warm_slots, members,
    )
    got = exchange(to_members, "member")
    to_groups = call(
        functools.partial(owner_kernel, warm_local, chunk, slot, groups),
        "owner",
        shape(groups * slot, width),
        (got.reshape(-1, width), cold_part, warm_list),
        2 * groups * slot * width * (hot_rows + warm_slots + cold_slots),
        vmem=16,
    )
    summands = exchange_rows(to_groups, 2)
    my_chunk, my_cold = call(
        functools.partial(finish_kernel, chunk, slot, ccap),
        "finish",
        (shape(groups * chunk, width), shape(cold_slots, width)),
        (summands,),
        2 * groups * slot * width * cold_slots,
    )
    chunks = exchange_rows(my_chunk, 4)
    warm_grad, to_all = call(
        spread_kernel,
        "spread",
        (shape(warm_local, width, kind=F32), shape(hot_each + cold_slots + EXTRA, width)),
        (chunks, my_cold, cold_list),
        2 * groups * slot * width,
    )
    last = lax.all_gather(to_all, "member", axis=0)
    hot_grad, cold_grad = call(
        functools.partial(last_kernel, groups, ccap),
        "last",
        (shape(hot_rows, width, kind=F32), shape(cold_local, width, kind=F32)),
        (last,),
        2 * cold_local * members * cold_slots * width,
    )
    return hot_grad, warm_grad, cold_grad


def solution(mesh):
    placed = (
        P(),
        P("member", None),
        P("group", None),
        P("group", "member", None, None),
        P("group", "member", None, None),
        P(("group", "member"), None),
        P(("group", "member")),
        P(),
        P(),
        P(),
        P(),
        P(),
        P(),
    )
    return jax.shard_map(
        per_device,
        mesh=mesh,
        in_specs=placed,
        out_specs=(P(), P("member", None), P("group", None)),
        check_vma=False,
    )
```

```python
import functools

import jax
import jax.numpy as jnp
from jax import lax
from jax.experimental import pallas as pl
from jax.experimental.pallas import tpu as pltpu
from jax.sharding import PartitionSpec as P

F32 = jnp.float32
BF16 = jnp.bfloat16
VMEM = pl.BlockSpec(memory_space=pltpu.VMEM)
HBM = pl.BlockSpec(memory_space=pltpu.HBM)
TILE = 512
LANES = 128
EXTRA = 16


def up(value, step):
    return (value + step - 1) // step * step


def iota(shape, axis):
    return lax.broadcasted_iota(jnp.int32, shape, axis)


def hits(left, right):
    return jnp.where(left == right, 1.0, 0.0).astype(BF16)


def short_hits(left, right):
    met = left.astype(jnp.int16) == right.astype(jnp.int16)
    return jnp.where(met, jnp.ones((), BF16), jnp.zeros((), BF16))


def dot(a, b):
    return jnp.dot(a, b, preferred_element_type=F32)


def dot_nt(a, b):
    return lax.dot_general(a, b, (((1,), (1,)), ((), ())), preferred_element_type=F32)


def column_of(row):
    size = row.shape[1]
    same = iota((size, size), 0) == iota((size, size), 1)
    return jnp.sum(jnp.where(same, row, 0), axis=1, keepdims=True)


def standing(ids_ref):
    fields, batch = ids_ref.shape
    filled = jnp.concatenate([ids_ref[...], jnp.zeros((LANES - fields, batch), jnp.int32)], axis=0)
    return filled.T


def field_column(stood, field):
    return jnp.sum(jnp.where(iota(stood.shape, 1) == field, stood, 0), axis=1, keepdims=True)


def columns(step):
    return pl.ds(step * TILE if isinstance(step, int) else pl.multiple_of(step * TILE, TILE), TILE)


def lookup_kernel(hot_ref, warm_ref, ids_ref, out_ref, table, stood_ref):
    rows, width = table.shape
    hot_rows = hot_ref.shape[0]
    table[0:hot_rows, :] = hot_ref[...]
    table[hot_rows:, :] = warm_ref[...]
    batch = ids_ref.shape[1]
    stood_ref[...] = standing(ids_ref)

    @pl.loop(0, out_ref.shape[1] // TILE, unroll=True)
    def _(step):
        pieces = []
        for k in range(TILE // width):
            ids = field_column(stood_ref[...], step * (TILE // width) + k)
            chosen = short_hits(iota((batch, rows), 1), ids)
            pieces.append(dot(chosen, table[...]).astype(BF16))
        out_ref[:, columns(step)] = jnp.concatenate(pieces, axis=1)


def tower_kernel(
    hot_rows, warm_rows,
    found_ref, cold_ref, ids_ref, label_ref, bias_ref, b_in_ref, w_out_ref, v_hbm, u_hbm, w_hbm,
    member_ref, cold_out_ref,
    stood_ref, inputs, crossed, d_layer, narrow, preact, total, v_ref, u_ref, w_ref, sems,
):
    v_copy = pltpu.make_async_copy(v_hbm, v_ref, sems.at[0])
    u_copy = pltpu.make_async_copy(u_hbm, u_ref, sems.at[1])
    w_copies = [
        pltpu.make_async_copy(w_hbm.at[pl.ds(at, TILE), :], w_ref.at[pl.ds(at, TILE), :], sems.at[2 + at // TILE])
        for at in range(0, w_ref.shape[0], TILE)
    ]
    for copy in (v_copy, u_copy, *w_copies):
        copy.start()
    fields, batch = ids_ref.shape
    width = cold_ref.shape[1]
    steps = inputs.shape[1] // TILE
    each = TILE // width
    cold_rows = cold_ref.shape[0]
    slots = hot_rows + warm_rows + cold_rows
    stood_ref[...] = standing(ids_ref)
    narrow[...] = jnp.zeros_like(narrow)
    v_copy.wait()

    @pl.loop(0, steps, unroll=True)
    def _(step):
        pieces = []
        for k in range(each):
            ids = field_column(stood_ref[...], step * each + k)
            chosen = short_hits(iota((batch, cold_rows), 1) + (slots - cold_rows), ids)
            pieces.append(dot(chosen, cold_ref[...]))
        fetched = jnp.concatenate(pieces, axis=1)
        part = (found_ref[:, columns(step)].astype(F32) + fetched).astype(BF16)
        inputs[:, columns(step)] = part
        narrow[...] += dot(part, v_ref[columns(step), :])

    low = narrow[...].astype(BF16)
    preact[...] = jnp.zeros_like(preact)
    u_copy.wait()

    for step in range(steps):
        w_copies[step].wait()
        part = inputs[:, columns(step)].astype(F32)
        cross = dot(low, u_ref[:, columns(step)]) + bias_ref[:, columns(step)]
        crossed[:, columns(step)] = cross
        layer_one = (part * cross + part).astype(BF16)
        preact[...] += dot(layer_one, w_ref[columns(step), :])

    pre = preact[...] + b_in_ref[...]
    gate = jax.nn.sigmoid(pre)
    w_out = w_out_ref[...].astype(F32)
    hidden = (pre * gate).astype(BF16).astype(F32)
    logits = jnp.sum(hidden * w_out, axis=1, keepdims=True)
    d_logit = jax.nn.sigmoid(logits) - column_of(label_ref[...].astype(F32))
    d_hidden = (d_logit * w_out * gate * (1.0 + pre * (1.0 - gate))).astype(BF16)
    narrow[...] = jnp.zeros_like(narrow)

    @pl.loop(0, steps, unroll=True)
    def _(step):
        part = inputs[:, columns(step)].astype(F32)
        d_part = dot_nt(d_hidden, w_ref[columns(step), :])
        d_layer[:, columns(step)] = d_part
        d_crossed = (d_part * part).astype(BF16)
        narrow[...] += dot_nt(d_crossed, u_ref[:, columns(step)])

    d_low = narrow[...].astype(BF16)
    total[...] = jnp.zeros_like(total)

    @pl.loop(0, steps, unroll=True)
    def _(step):
        d_in = d_layer[:, columns(step)] * (crossed[:, columns(step)] + 1.0)
        d_in += dot_nt(d_low, v_ref[columns(step), :])
        high = d_in.astype(BF16)
        for k in range(each):
            ids = field_column(stood_ref[...], step * each + k)
            piece = slice(k * width, (k + 1) * width)
            value = high[:, piece]
            total[...] += lax.dot_general(value, short_hits(iota((batch, slots), 1), ids), (((0,), (0,)), ((), ())), preferred_element_type=F32)

    members = member_ref.shape[0]
    hot_each = hot_rows // members
    warm_each = warm_rows // members

    turned = total[...].T

    def rows(start, size):
        return turned[start : start + size, :].astype(BF16)

    for m in range(members):
        member_ref[m, 0:hot_each, :] = rows(m * hot_each, hot_each)
        member_ref[m, hot_each : hot_each + warm_each, :] = rows(hot_rows + m * warm_each, warm_each)
    cold_out_ref[...] = rows(hot_rows + warm_rows, cold_rows)


def call(kernel, name, out_shape, args, flops, scratch=(), vmem=8, transcendentals=0, apart=0):
    single = isinstance(out_shape, jax.ShapeDtypeStruct)
    return pl.pallas_call(
        kernel,
        name=name,
        out_shape=out_shape,
        in_specs=[VMEM] * (len(args) - apart) + [HBM] * apart,
        out_specs=VMEM if single else tuple(VMEM for _ in out_shape),
        scratch_shapes=list(scratch),
        compiler_params=pltpu.CompilerParams(vmem_limit_bytes=vmem * 2**20),
        cost_estimate=pl.CostEstimate(flops=flops, bytes_accessed=2_000_000, transcendentals=transcendentals),
    )(*args)


def lookup(hot, warm, ids):
    fields, batch = ids.shape
    width = hot.shape[1]
    rows = hot.shape[0] + warm.shape[0]
    return call(
        lookup_kernel, "lookup", jax.ShapeDtypeStruct((batch, fields * width), BF16), (hot, warm, ids),
        4 * batch * fields * rows * width,
        [pltpu.VMEM((rows, width), BF16), pltpu.VMEM((batch, LANES), jnp.int32)], 16,
    )


def tower(found, cold, ids, labels, bias, b_in, w_out, v, u, w, hot_rows, warm_rows, members):
    fields, batch = ids.shape
    width = cold.shape[1]
    wide, rank = v.shape
    hid = w.shape[1]
    slots = hot_rows + warm_rows + cold.shape[0]
    each = (hot_rows + warm_rows) // members
    flops = 2 * batch * wide * (2 * rank + hid) * 2 + 4 * batch * fields * slots * width * 2
    return call(
        functools.partial(tower_kernel, hot_rows, warm_rows),
        "tower",
        (
            jax.ShapeDtypeStruct((members, each, width), BF16),
            jax.ShapeDtypeStruct(cold.shape, BF16),
        ),
        (found, cold, ids, labels, bias, b_in, w_out, v, u, w),
        flops,
        [
            pltpu.VMEM((batch, LANES), jnp.int32),
            pltpu.VMEM((batch, wide), BF16),
            pltpu.VMEM((batch, wide), F32),
            pltpu.VMEM((batch, wide), F32),
            pltpu.VMEM((batch, rank), F32),
            pltpu.VMEM((batch, hid), F32),
            pltpu.VMEM((width, slots), F32),
            pltpu.VMEM(v.shape, BF16),
            pltpu.VMEM(u.shape, BF16),
            pltpu.VMEM(w.shape, BF16),
            pltpu.SemaphoreType.DMA((2 + wide // TILE,)),
        ],
        52,
        batch * hid,
        3,
    )


def serve_cold_kernel(table_ref, list_ref, out_ref):
    ccap, groups = list_ref.shape
    shape = (out_ref.shape[0], groups)
    row, group = iota(shape, 0), iota(shape, 1)
    ids = jnp.zeros(shape, jnp.int32)
    for k in range(ccap):
        ids = jnp.where((row // ccap == group) & (row % ccap == k), list_ref[k : k + 1, :], ids)
    ids = jnp.sum(ids, axis=1, keepdims=True)
    out_ref[...] = dot(short_hits(iota((shape[0], table_ref.shape[0]), 1), ids), table_ref[...]).astype(BF16)


def serve_warm_kernel(table_ref, list_ref, out_ref):
    members, wcap = list_ref.shape
    for m in range(members):
        ids = column_of(list_ref[m : m + 1, :])
        out_ref[m] = dot(short_hits(iota((wcap, table_ref.shape[0]), 1), ids), table_ref[...]).astype(BF16)


def owner_kernel(warm_local, chunk, slot, groups, got_ref, cold_ref, list_ref, out_ref):
    out_rows = groups * slot
    members = list_ref.shape[0]
    keep = cold_ref.shape[0]
    keeps = keep // groups
    hot_each = got_ref.shape[0] // members - list_ref.shape[1]
    hot_to = warm_local + iota((1, hot_each), 1)
    to = jnp.concatenate([piece for m in range(members) for piece in (hot_to, list_ref[m : m + 1, :])], axis=1)
    place = iota((out_rows, 1), 0)
    group, at = place // slot, place % slot
    wanted = jnp.where(at < chunk, group * chunk + at, -1)
    cold_wanted = jnp.where((at >= chunk) & (at < chunk + keeps), group * keeps + at - chunk, -1)
    out = dot(hits(wanted, to), got_ref[...])
    out += dot(hits(cold_wanted, iota((out_rows, keep), 1)), cold_ref[...])
    out_ref[...] = out.astype(BF16)


def finish_kernel(chunk, slot, got_ref, list_ref, chunk_ref, cold_ref):
    total_rows = got_ref.shape[0]
    groups = total_rows // slot
    rows = up(chunk, 16)
    shape = (rows, total_rows)
    own = jnp.where(iota(shape, 0) < chunk, iota(shape, 0), -1)
    summed = dot(hits(own, iota(shape, 1) % slot), got_ref[...]).astype(BF16)
    place = iota((groups * chunk, rows), 0) % chunk
    chunk_ref[...] = dot(hits(place, iota((groups * chunk, rows), 1)), summed).astype(BF16)
    ccap = list_ref.shape[0]
    cold_rows, width = groups * ccap, cold_ref.shape[1]
    row = iota((cold_rows, 1), 0)
    wanted = row % groups * slot + chunk + row // groups
    picked = dot(hits(wanted, iota((cold_rows, total_rows), 1)), got_ref[...])
    cold_ref[0:cold_rows, :] = picked.astype(BF16)
    code = jnp.zeros((EXTRA, groups), jnp.int32)
    row = iota((EXTRA, groups), 0)
    for k in range(ccap):
        code = jnp.where(row == 2 * k, list_ref[k : k + 1, :] // 32, code)
        code = jnp.where(row == 2 * k + 1, list_ref[k : k + 1, :] % 32, code)
    code = jnp.concatenate([code.astype(F32), jnp.zeros((EXTRA, width - groups), F32)], axis=1)
    cold_ref[cold_rows:, :] = code.astype(BF16)


def cold_kernel(groups, ccap, got_ref, cold_ref):
    members, each, width = got_ref.shape
    cold_local = cold_ref.shape[0]
    last_row = each - EXTRA
    total = jnp.zeros((cold_local, width), F32)
    for m in range(members):
        code = got_ref[m, last_row:, :].astype(F32)
        to = [code[2 * k : 2 * k + 1, :groups] * 32.0 + code[2 * k + 1 : 2 * k + 2, :groups] for k in range(ccap)]
        to = jnp.concatenate(to, axis=1).astype(jnp.int32)
        total += dot(short_hits(iota((cold_local, to.shape[1]), 0), to), got_ref[m, 0:last_row, :])
    cold_ref[...] = total


def share_kernel(start, got_ref, out_ref):
    members, rows, _ = out_ref.shape
    for m in range(members):
        out_ref[m] = got_ref[start : start + rows, :]


def widen_kernel(got_ref, out_ref):
    out_ref[...] = got_ref[0 : out_ref.shape[0], :].astype(F32)


def per_device(
    hot_table, warm_table, cold_table, warm_serve, cold_serve, feature_ids, labels,
    cross_v, cross_u, cross_bias, w_in, b_in, w_out,
):
    width = hot_table.shape[1]
    hot_rows = hot_table.shape[0]
    warm_local = warm_table.shape[0]
    cold_local = cold_table.shape[0]
    warm_list = warm_serve[0, 0]
    cold_list = cold_serve[0, 0].T
    ids = feature_ids.T
    members, wcap = warm_list.shape
    ccap, groups = cold_list.shape
    warm_slots = members * wcap
    cold_slots = groups * ccap
    hot_each = hot_rows // members
    chunk = up(up(warm_local + hot_each, groups) // groups, 4)
    slot = up(chunk + ccap, 2)

    def exchange(x, axis):
        return lax.all_to_all(x, axis, split_axis=0, concat_axis=0, tiled=True)

    def exchange_rows(x, tile):
        parts = x.reshape(x.shape[0] // tile, tile, width)
        return exchange(parts, "group").reshape(x.shape)

    def shape(*dims, kind=BF16):
        return jax.ShapeDtypeStruct(dims, kind)

    cold_wanted = call(
        serve_cold_kernel, "serve_cold", shape(cold_slots, width), (cold_table, cold_list),
        2 * cold_slots * cold_local * width,
    )
    cold_fetched = exchange_rows(cold_wanted, ccap)
    warm_wanted = call(
        serve_warm_kernel, "serve_warm", shape(members, wcap, width), (warm_table, warm_list),
        2 * warm_slots * warm_local * width,
    )
    warm_fetched = exchange(warm_wanted, "member").reshape(warm_slots, width)
    found = lookup(hot_table, warm_fetched, ids)
    to_members, cold_part = tower(
        found, cold_fetched, ids, labels.reshape(1, -1),
        cross_bias.reshape(1, -1), b_in.reshape(1, -1), w_out.reshape(1, -1),
        cross_v, cross_u, w_in, hot_rows, warm_slots, members,
    )
    got = exchange(to_members, "member")
    to_groups = call(
        functools.partial(owner_kernel, warm_local, chunk, slot, groups),
        "owner",
        shape(groups * slot, width),
        (got.reshape(-1, width), cold_part, warm_list),
        2 * groups * slot * width * (hot_rows + warm_slots + cold_slots),
        vmem=16,
    )
    summands = exchange_rows(to_groups, 2)
    my_chunk, my_cold = call(
        functools.partial(finish_kernel, chunk, slot),
        "finish",
        (shape(groups * chunk, width), shape(cold_slots + EXTRA, width)),
        (summands, cold_list),
        2 * groups * slot * width * cold_slots,
    )
    chunks = exchange_rows(my_chunk, 4)
    all_cold = lax.all_gather(my_cold, "member", axis=0)
    chunks, all_cold = lax.optimization_barrier((chunks, all_cold))
    cold_grad = call(
        functools.partial(cold_kernel, groups, ccap),
        "cold",
        shape(cold_local, width, kind=F32),
        (all_cold,),
        2 * cold_local * members * cold_slots * width,
    )
    my_hot = call(
        functools.partial(share_kernel, warm_local), "share", shape(members, hot_each, width), (chunks,), hot_rows * width
    )
    all_hot = exchange(my_hot, "member")
    warm_grad = call(widen_kernel, "warm", shape(warm_local, width, kind=F32), (chunks,), warm_local * width)
    hot_grad = call(widen_kernel, "hot", shape(hot_rows, width, kind=F32), (all_hot.reshape(hot_rows, width),), hot_rows * width)
    return hot_grad, warm_grad, cold_grad


def solution(mesh):
    placed = (
        P(),
        P("member", None),
        P("group", None),
        P("group", "member", None, None),
        P("group", "member", None, None),
        P(("group", "member"), None),
        P(("group", "member")),
        P(),
        P(),
        P(),
        P(),
        P(),
        P(),
    )
    return jax.shard_map(
        per_device,
        mesh=mesh,
        in_specs=placed,
        out_specs=(P(), P("member", None), P("group", None)),
        check_vma=False,
    )
```

```python
import functools

import jax
import jax.numpy as jnp
from jax import lax
from jax.experimental import pallas as pl
from jax.experimental.pallas import tpu as pltpu
from jax.sharding import PartitionSpec as P

F32 = jnp.float32
BF16 = jnp.bfloat16
VMEM = pl.BlockSpec(memory_space=pltpu.VMEM)
HBM = pl.BlockSpec(memory_space=pltpu.HBM)
TILE = 1280
LANES = 128
EXTRA = 16


def up(value, step):
    return (value + step - 1) // step * step


def iota(shape, axis):
    return lax.broadcasted_iota(jnp.int32, shape, axis)


def hits(left, right):
    return jnp.where(left == right, 1.0, 0.0).astype(BF16)


def short_hits(left, right):
    met = left.astype(jnp.int16) == right.astype(jnp.int16)
    return jnp.where(met, jnp.ones((), BF16), jnp.zeros((), BF16))


def dot(a, b):
    return jnp.dot(a, b, preferred_element_type=F32)


def dot_nt(a, b):
    return lax.dot_general(a, b, (((1,), (1,)), ((), ())), preferred_element_type=F32)


def column_of(row):
    size = row.shape[1]
    same = iota((size, size), 0) == iota((size, size), 1)
    return jnp.sum(jnp.where(same, row, 0), axis=1, keepdims=True)


def standing(ids_ref):
    fields, batch = ids_ref.shape
    filled = jnp.concatenate([ids_ref[...], jnp.zeros((LANES - fields, batch), jnp.int32)], axis=0)
    return filled.T


def field_column(stood, field):
    return jnp.sum(jnp.where(iota(stood.shape, 1) == field, stood, 0), axis=1, keepdims=True)


def columns(step):
    return pl.ds(step * TILE if isinstance(step, int) else pl.multiple_of(step * TILE, TILE), TILE)


def lookup_kernel(hot_ref, warm_ref, ids_ref, out_ref, table, stood_ref):
    rows, width = table.shape
    hot_rows = hot_ref.shape[0]
    table[0:hot_rows, :] = hot_ref[...]
    table[hot_rows:, :] = warm_ref[...]
    batch = ids_ref.shape[1]
    stood_ref[...] = standing(ids_ref)

    @pl.loop(0, out_ref.shape[1] // TILE, unroll=True)
    def _(step):
        pieces = []
        for k in range(TILE // width):
            ids = field_column(stood_ref[...], step * (TILE // width) + k)
            chosen = short_hits(iota((batch, rows), 1), ids)
            pieces.append(dot(chosen, table[...]).astype(BF16))
        out_ref[:, columns(step)] = jnp.concatenate(pieces, axis=1)


def tower_kernel(
    hot_rows, warm_rows,
    found_ref, cold_ref, ids_ref, label_ref, bias_ref, b_in_ref, w_out_ref, v_hbm, u_hbm, w_hbm,
    member_ref, cold_out_ref,
    stood_ref, inputs, crossed, d_layer, narrow, preact, total, v_ref, u_ref, w_ref, sems,
):
    v_copy = pltpu.make_async_copy(v_hbm, v_ref, sems.at[0])
    u_copy = pltpu.make_async_copy(u_hbm, u_ref, sems.at[1])
    w_copies = [
        pltpu.make_async_copy(w_hbm.at[pl.ds(at, TILE), :], w_ref.at[pl.ds(at, TILE), :], sems.at[2 + at // TILE])
        for at in range(0, w_ref.shape[0], TILE)
    ]
    for copy in (v_copy, u_copy, *w_copies):
        copy.start()
    fields, batch = ids_ref.shape
    width = cold_ref.shape[1]
    steps = inputs.shape[1] // TILE
    each = TILE // width
    cold_rows = cold_ref.shape[0]
    slots = hot_rows + warm_rows + cold_rows
    stood_ref[...] = standing(ids_ref)
    narrow[...] = jnp.zeros_like(narrow)
    v_copy.wait()

    @pl.loop(0, steps, unroll=True)
    def _(step):
        pieces = []
        for k in range(each):
            ids = field_column(stood_ref[...], step * each + k)
            chosen = short_hits(iota((batch, cold_rows), 1) + (slots - cold_rows), ids)
            pieces.append(dot(chosen, cold_ref[...]))
        fetched = jnp.concatenate(pieces, axis=1)
        part = (found_ref[:, columns(step)].astype(F32) + fetched).astype(BF16)
        inputs[:, columns(step)] = part
        narrow[...] += dot(part, v_ref[columns(step), :])

    low = narrow[...].astype(BF16)
    preact[...] = jnp.zeros_like(preact)
    u_copy.wait()

    for step in range(steps):
        w_copies[step].wait()
        part = inputs[:, columns(step)].astype(F32)
        cross = dot(low, u_ref[:, columns(step)]) + bias_ref[:, columns(step)]
        crossed[:, columns(step)] = cross
        layer_one = (part * cross + part).astype(BF16)
        preact[...] += dot(layer_one, w_ref[columns(step), :])

    pre = preact[...] + b_in_ref[...]
    gate = jax.nn.sigmoid(pre)
    w_out = w_out_ref[...].astype(F32)
    hidden = (pre * gate).astype(BF16).astype(F32)
    logits = jnp.sum(hidden * w_out, axis=1, keepdims=True)
    d_logit = jax.nn.sigmoid(logits) - column_of(label_ref[...].astype(F32))
    d_hidden = (d_logit * w_out * gate * (1.0 + pre * (1.0 - gate))).astype(BF16)
    narrow[...] = jnp.zeros_like(narrow)

    @pl.loop(0, steps, unroll=True)
    def _(step):
        part = inputs[:, columns(step)].astype(F32)
        d_part = dot_nt(d_hidden, w_ref[columns(step), :])
        d_layer[:, columns(step)] = d_part
        d_crossed = (d_part * part).astype(BF16)
        narrow[...] += dot_nt(d_crossed, u_ref[:, columns(step)])

    d_low = narrow[...].astype(BF16)
    total[...] = jnp.zeros_like(total)

    @pl.loop(0, steps, unroll=True)
    def _(step):
        d_in = d_layer[:, columns(step)] * (crossed[:, columns(step)] + 1.0)
        d_in += dot_nt(d_low, v_ref[columns(step), :])
        high = d_in.astype(BF16)
        for k in range(each):
            ids = field_column(stood_ref[...], step * each + k)
            piece = slice(k * width, (k + 1) * width)
            value = high[:, piece]
            total[...] += lax.dot_general(value, short_hits(iota((batch, slots), 1), ids), (((0,), (0,)), ((), ())), preferred_element_type=F32)

    members = member_ref.shape[0]
    hot_each = hot_rows // members
    warm_each = warm_rows // members

    turned = total[...].T

    def rows(start, size):
        return turned[start : start + size, :].astype(BF16)

    for m in range(members):
        member_ref[m, 0:hot_each, :] = rows(m * hot_each, hot_each)
        member_ref[m, hot_each : hot_each + warm_each, :] = rows(hot_rows + m * warm_each, warm_each)
    cold_out_ref[...] = rows(hot_rows + warm_rows, cold_rows)


def call(kernel, name, out_shape, args, flops, scratch=(), vmem=8, transcendentals=0, apart=0):
    single = isinstance(out_shape, jax.ShapeDtypeStruct)
    return pl.pallas_call(
        kernel,
        name=name,
        out_shape=out_shape,
        in_specs=[VMEM] * (len(args) - apart) + [HBM] * apart,
        out_specs=VMEM if single else tuple(VMEM for _ in out_shape),
        scratch_shapes=list(scratch),
        compiler_params=pltpu.CompilerParams(vmem_limit_bytes=vmem * 2**20),
        cost_estimate=pl.CostEstimate(flops=flops, bytes_accessed=2_000_000, transcendentals=transcendentals),
    )(*args)


def lookup(hot, warm, ids):
    fields, batch = ids.shape
    width = hot.shape[1]
    rows = hot.shape[0] + warm.shape[0]
    return call(
        lookup_kernel, "lookup", jax.ShapeDtypeStruct((batch, fields * width), BF16), (hot, warm, ids),
        4 * batch * fields * rows * width,
        [pltpu.VMEM((rows, width), BF16), pltpu.VMEM((batch, LANES), jnp.int32)], 16,
    )


def tower(found, cold, ids, labels, bias, b_in, w_out, v, u, w, hot_rows, warm_rows, members):
    fields, batch = ids.shape
    width = cold.shape[1]
    wide, rank = v.shape
    hid = w.shape[1]
    slots = hot_rows + warm_rows + cold.shape[0]
    each = (hot_rows + warm_rows) // members
    flops = 2 * batch * wide * (2 * rank + hid) * 2 + 4 * batch * fields * slots * width * 2
    return call(
        functools.partial(tower_kernel, hot_rows, warm_rows),
        "tower",
        (
            jax.ShapeDtypeStruct((members, each, width), BF16),
            jax.ShapeDtypeStruct(cold.shape, BF16),
        ),
        (found, cold, ids, labels, bias, b_in, w_out, v, u, w),
        flops,
        [
            pltpu.VMEM((batch, LANES), jnp.int32),
            pltpu.VMEM((batch, wide), BF16),
            pltpu.VMEM((batch, wide), F32),
            pltpu.VMEM((batch, wide), F32),
            pltpu.VMEM((batch, rank), F32),
            pltpu.VMEM((batch, hid), F32),
            pltpu.VMEM((width, slots), F32),
            pltpu.VMEM(v.shape, BF16),
            pltpu.VMEM(u.shape, BF16),
            pltpu.VMEM(w.shape, BF16),
            pltpu.SemaphoreType.DMA((2 + wide // TILE,)),
        ],
        52,
        batch * hid,
        3,
    )


def serve_cold_kernel(table_ref, list_ref, out_ref, code_ref):
    ccap, groups = list_ref.shape
    shape = (out_ref.shape[0], groups)
    row, group = iota(shape, 0), iota(shape, 1)
    ids = jnp.zeros(shape, jnp.int32)
    for k in range(ccap):
        ids = jnp.where((row // ccap == group) & (row % ccap == k), list_ref[k : k + 1, :], ids)
    ids = jnp.sum(ids, axis=1, keepdims=True)
    out_ref[...] = dot(short_hits(iota((shape[0], table_ref.shape[0]), 1), ids), table_ref[...]).astype(BF16)
    code = jnp.zeros((EXTRA, groups), jnp.int32)
    row = iota((EXTRA, groups), 0)
    for k in range(ccap):
        code = jnp.where(row == 2 * k, list_ref[k : k + 1, :] // 32, code)
        code = jnp.where(row == 2 * k + 1, list_ref[k : k + 1, :] % 32, code)
    code = jnp.concatenate([code.astype(F32), jnp.zeros((EXTRA, code_ref.shape[1] - groups), F32)], axis=1)
    code_ref[...] = code.astype(BF16)


def serve_warm_kernel(list_hbm, table_hbm, out_ref, list_ref, table_ref, sems):
    list_copy = pltpu.make_async_copy(list_hbm, list_ref, sems.at[0])
    table_copy = pltpu.make_async_copy(table_hbm, table_ref, sems.at[1])
    list_copy.start()
    table_copy.start()
    list_copy.wait()
    members, wcap = list_ref.shape
    found = [short_hits(iota((wcap, table_ref.shape[0]), 1), column_of(list_ref[m : m + 1, :])) for m in range(members)]
    table_copy.wait()
    for m in range(members):
        out_ref[m] = dot(found[m], table_ref[...]).astype(BF16)


def owner_kernel(warm_local, chunk, slot, groups, got_ref, cold_ref, list_ref, out_ref):
    out_rows = groups * slot
    members = list_ref.shape[0]
    keep = cold_ref.shape[0]
    keeps = keep // groups
    hot_each = got_ref.shape[0] // members - list_ref.shape[1]
    hot_to = warm_local + iota((1, hot_each), 1)
    to = jnp.concatenate([piece for m in range(members) for piece in (hot_to, list_ref[m : m + 1, :])], axis=1)
    place = iota((out_rows, 1), 0)
    group, at = place // slot, place % slot
    wanted = jnp.where(at < chunk, group * chunk + at, -1)
    cold_wanted = jnp.where((at >= chunk) & (at < chunk + keeps), group * keeps + at - chunk, -1)
    out = dot(hits(wanted, to), got_ref[...])
    out += dot(hits(cold_wanted, iota((out_rows, keep), 1)), cold_ref[...])
    out_ref[...] = out.astype(BF16)


def finish_kernel(chunk, slot, ccap, got_ref, code_ref, chunk_ref, cold_ref):
    total_rows = got_ref.shape[0]
    groups = total_rows // slot
    rows = up(chunk, 16)
    shape = (rows, total_rows)
    own = jnp.where(iota(shape, 0) < chunk, iota(shape, 0), -1)
    summed = dot(hits(own, iota(shape, 1) % slot), got_ref[...]).astype(BF16)
    place = iota((groups * chunk, rows), 0) % chunk
    chunk_ref[...] = dot(hits(place, iota((groups * chunk, rows), 1)), summed).astype(BF16)
    cold_rows = groups * ccap
    row = iota((cold_rows, 1), 0)
    wanted = row % groups * slot + chunk + row // groups
    picked = dot(hits(wanted, iota((cold_rows, total_rows), 1)), got_ref[...])
    cold_ref[0:cold_rows, :] = picked.astype(BF16)
    cold_ref[cold_rows:, :] = code_ref[...]


def cold_kernel(groups, ccap, got_ref, cold_ref):
    members, each, width = got_ref.shape
    cold_local = cold_ref.shape[0]
    last_row = each - EXTRA
    total = jnp.zeros((cold_local, width), F32)
    for m in range(members):
        code = got_ref[m, last_row:, :].astype(F32)
        to = [code[2 * k : 2 * k + 1, :groups] * 32.0 + code[2 * k + 1 : 2 * k + 2, :groups] for k in range(ccap)]
        to = jnp.concatenate(to, axis=1).astype(jnp.int32)
        total += dot(short_hits(iota((cold_local, to.shape[1]), 0), to), got_ref[m, 0:last_row, :])
    cold_ref[...] = total


def share_kernel(start, got_ref, out_ref):
    members, rows, _ = out_ref.shape
    for m in range(members):
        out_ref[m] = got_ref[start : start + rows, :]


def widen_kernel(got_ref, out_ref):
    out_ref[...] = got_ref[0 : out_ref.shape[0], :].astype(F32)


def per_device(
    hot_table, warm_table, cold_table, warm_serve, cold_serve, feature_ids, labels,
    cross_v, cross_u, cross_bias, w_in, b_in, w_out,
):
    width = hot_table.shape[1]
    hot_rows = hot_table.shape[0]
    warm_local = warm_table.shape[0]
    cold_local = cold_table.shape[0]
    warm_list = warm_serve[0, 0]
    cold_list = cold_serve[0, 0].T
    ids = feature_ids.T
    members, wcap = warm_list.shape
    ccap, groups = cold_list.shape
    warm_slots = members * wcap
    cold_slots = groups * ccap
    hot_each = hot_rows // members
    chunk = up(up(warm_local + hot_each, groups) // groups, 4)
    slot = up(chunk + ccap, 2)

    def exchange(x, axis):
        return lax.all_to_all(x, axis, split_axis=0, concat_axis=0, tiled=True)

    def exchange_rows(x, tile):
        parts = x.reshape(x.shape[0] // tile, tile, width)
        return exchange(parts, "group").reshape(x.shape)

    def shape(*dims, kind=BF16):
        return jax.ShapeDtypeStruct(dims, kind)

    cold_wanted, code = call(
        serve_cold_kernel, "serve_cold", (shape(cold_slots, width), shape(EXTRA, width)), (cold_table, cold_list),
        2 * cold_slots * cold_local * width,
    )
    cold_fetched = exchange_rows(cold_wanted, ccap)
    warm_wanted = call(
        serve_warm_kernel, "serve_warm", shape(members, wcap, width), (warm_list, warm_table),
        2 * warm_slots * warm_local * width,
        [
            pltpu.VMEM((members, wcap), jnp.int32),
            pltpu.VMEM((warm_local, width), BF16),
            pltpu.SemaphoreType.DMA((2,)),
        ],
        60,
        apart=2,
    )
    warm_fetched = exchange(warm_wanted, "member").reshape(warm_slots, width)
    found = lookup(hot_table, warm_fetched, ids)
    to_members, cold_part = tower(
        found, cold_fetched, ids, labels.reshape(1, -1),
        cross_bias.reshape(1, -1), b_in.reshape(1, -1), w_out.reshape(1, -1),
        cross_v, cross_u, w_in, hot_rows, warm_slots, members,
    )
    got = exchange(to_members, "member")
    to_groups = call(
        functools.partial(owner_kernel, warm_local, chunk, slot, groups),
        "owner",
        shape(groups * slot, width),
        (got.reshape(-1, width), cold_part, warm_list),
        2 * groups * slot * width * (hot_rows + warm_slots + cold_slots),
        vmem=16,
    )
    summands = exchange_rows(to_groups, 2)
    my_chunk, my_cold = call(
        functools.partial(finish_kernel, chunk, slot, ccap),
        "finish",
        (shape(groups * chunk, width), shape(cold_slots + EXTRA, width)),
        (summands, code),
        2 * groups * slot * width * cold_slots,
    )
    chunks = exchange_rows(my_chunk, 4)
    all_cold = lax.all_gather(my_cold, "member", axis=0)
    chunks, all_cold = lax.optimization_barrier((chunks, all_cold))
    cold_grad = call(
        functools.partial(cold_kernel, groups, ccap),
        "cold",
        shape(cold_local, width, kind=F32),
        (all_cold,),
        2 * cold_local * members * cold_slots * width,
    )
    my_hot = call(
        functools.partial(share_kernel, warm_local), "share", shape(members, hot_each, width), (chunks,), hot_rows * width
    )
    all_hot = exchange(my_hot, "member")
    warm_grad = call(widen_kernel, "warm", shape(warm_local, width, kind=F32), (chunks,), warm_local * width)
    hot_grad = call(widen_kernel, "hot", shape(hot_rows, width, kind=F32), (all_hot.reshape(hot_rows, width),), hot_rows * width)
    return hot_grad, warm_grad, cold_grad


def solution(mesh):
    placed = (
        P(),
        P("member", None),
        P("group", None),
        P("group", "member", None, None),
        P("group", "member", None, None),
        P(("group", "member"), None),
        P(("group", "member")),
        P(),
        P(),
        P(),
        P(),
        P(),
        P(),
    )
    return jax.shard_map(
        per_device,
        mesh=mesh,
        in_specs=placed,
        out_specs=(P(), P("member", None), P("group", None)),
        check_vma=False,
    )
```
